256 devices in a mesh: section: 8 (over y_lo, x), dp: 8 (over z), tensor: 4 (over y_hi, core).
Axes of the slice: x: 4, y: 4 (y_hi: 2, y_lo: 2; y = y_hi * 2 + y_lo), z: 8, core: 2. Of those that a mesh axis runs over, the one named last changes fastest.
Arguments:
- rollout: bfloat16 [16, 256, 5120], P('dp', 'tensor'), may hold values from -6 to 6
- document_ids: int32 [16, 256], P('dp'), may hold values from 0 to 31, never falling along the last dimension, each value on 1 to 128 neighbouring positions
- batch_order: int32 [8, 2], P('dp'), may hold values from 0 to 1, each once within a row
- gains: float32 [8, 5120], P('section'), may hold values from 0.25 to 1.75
- w_query: bfloat16 [8, 5120, 2560], P('section', None, 'tensor'), may hold values from -0.078125 to 0.078125
- bias_query: float32 [8, 2560], P('section', 'tensor'), may hold values from -3 to 3
- w_kv: bfloat16 [8, 2, 5120, 512], P('section', None, None, 'tensor'), may hold values from -0.078125 to 0.078125
- bias_value: float32 [8, 512], P('section', 'tensor'), may hold values from -3 to 3
- w_out: bfloat16 [8, 2560, 5120], P('section', 'tensor', 'dp'), may hold values from -0.125 to 0.125
Outputs:
- hidden_states: bfloat16 [8, 16, 256, 5120], P('section', 'dp', 'tensor')
The draws below stay inside these ranges and needn't reach their ends.
Inputs may be any that keep to these rules, and one draw needn't show every extreme that they name: `document_ids`: within each micro-batch the document numbers never fall. `batch_order`: each row holds every number of 0 to 1 once.
All inputs are finite; a program needn't handle non-finite values.
Results may differ from the reference program's by a relative error of at most 0.029.
Values may be sent and summed in bfloat16 or wider, within the bound.
A program may use at most 64 MiB of HBM per device.

```python
import math
import jax
import jax.numpy as jnp
import numpy as np
from jax import lax

D = 5120
HD = 128
HEADS = 20
KVH = 4
TOK = 256
MB_DEV = 2
MICRO = 16
LAYERS = 8
N_DP = 8


def level_of(rng, extent, shards, least, largest):
    loudness = 1.0
    for position, shards_of in shards:
        steps = jax.random.uniform(jax.random.fold_in(jax.random.fold_in(rng, 6), position), (shards_of,), jnp.float32, least / len(shards), largest / len(shards))
        loudness = loudness * jnp.repeat(jnp.exp(steps), extent[position] // shards_of).reshape((-1,) + (1,) * (len(extent) - 1 - position))
    return loudness


def length_profile(count, total, reach, lean):
    loads = [(1 << 20) // math.isqrt(standing ** lean) + 1 for standing in range(2, count + 1)]
    rest, holding = total - reach - (count - 1), [1] * (count - 1)
    while rest > 0:
        free = [i for i in range(count - 1) if holding[i] < reach]
        mass, left = sum([loads[i] for i in free]), rest
        for i in free:
            addition = min(reach - holding[i], max(1, left * loads[i] // mass), rest)
            holding[i] = holding[i] + addition
            rest = rest - addition
    return np.array([reach] + holding)


def uneven(stream_key, count, total, bound, slope):
    if count == 2:
        one = jax.random.randint(stream_key, (), max(1, total - bound), min(bound, total - 1) + 1)
        return jnp.stack([one, total - one])
    sizes = jnp.asarray(length_profile(count, total, bound, slope), jnp.int32)
    pairs = (count - 1) // 2
    giver, sink = sizes[1:1 + 2 * pairs:2], sizes[2:2 + 2 * pairs:2]
    margin = jnp.minimum(giver - 1, bound - sink)
    passed = jax.random.randint(jax.random.fold_in(stream_key, 1), (pairs,), 0, 1 << 20) % (margin + 1)
    sizes = sizes.at[1:1 + 2 * pairs:2].set(giver - passed).at[2:2 + 2 * pairs:2].set(sink + passed)
    return sizes[jax.random.permutation(jax.random.fold_in(stream_key, 2), count)]


def normal_values(rng, dims, width, limit, split=(), dtype=jnp.bfloat16):
    gain = level_of(rng, dims, split, -0.22, 0.18) if split else 1.0
    result = jax.random.normal(rng, dims, jnp.float32) * width * gain
    return jnp.minimum(jnp.maximum(result, -limit), limit).astype(dtype)


def setup_inputs(seed: int = 0) -> dict:
    key_of = jax.random.split(jax.random.key(seed), 10)
    rollout = normal_values(key_of[0], (MICRO, TOK, D), 1.0, 6.0, ((0, 8), (1, 4)))
    document_ids = jax.vmap(lambda own: jnp.searchsorted(jnp.cumsum(uneven(own, max(TOK // 8, 4), TOK, TOK // 2, 2)), jnp.arange(TOK), side="right"))(jax.random.split(key_of[1], MICRO)).reshape((MICRO, TOK)).astype(jnp.int32)
    batch_order = jax.vmap(lambda own: jax.random.permutation(own, MB_DEV))(jax.random.split(key_of[2], N_DP)).reshape((N_DP, MB_DEV)).astype(jnp.int32)
    gains = jnp.clip(1.0 + 0.15 * jax.random.normal(key_of[3], (LAYERS, D), jnp.float32), 0.25, 1.75)
    w_query = normal_values(key_of[4], (LAYERS, D, HEADS * HD), D ** -0.5, 0.078125, ((0, 8), (2, 4)))
    bias_query = normal_values(key_of[5], (LAYERS, HEADS * HD), 0.5, 3.0, ((0, 8), (1, 4)), jnp.float32)
    w_kv = normal_values(key_of[6], (LAYERS, 2, D, KVH * HD), D ** -0.5, 0.078125, ((0, 8), (3, 4)))
    bias_value = normal_values(key_of[7], (LAYERS, KVH * HD), 0.5, 3.0, ((0, 8), (1, 4)), jnp.float32)
    w_out = normal_values(key_of[8], (LAYERS, HEADS * HD, D), (HEADS * HD) ** -0.5, 0.125, ((0, 8), (1, 4), (2, 8)))
    return {"rollout": rollout, "document_ids": document_ids, "batch_order": batch_order, "gains": gains, "w_query": w_query, "bias_query": bias_query, "w_kv": w_kv, "bias_value": bias_value, "w_out": w_out}


def layer_apply(inputs, doc_row, gain_row, wq, bq, wk, wv, bv, wo):
    group = HEADS // KVH
    values = inputs.astype(jnp.float32)
    meansq = lax.optimization_barrier(jnp.mean(values * values, axis=-1, keepdims=True))
    normed = (values * lax.rsqrt(meansq + 1e-06) * gain_row).astype(jnp.bfloat16)
    query = (jnp.dot(normed, wq, preferred_element_type=jnp.float32) + bq).astype(jnp.bfloat16)
    keys = jnp.dot(normed, wk, preferred_element_type=jnp.float32).astype(jnp.bfloat16)
    vals = (jnp.dot(normed, wv, preferred_element_type=jnp.float32) + bv).astype(jnp.bfloat16)
    query_heads = query.reshape(TOK, KVH, group, HD).astype(jnp.float32)
    key_heads = keys.reshape(TOK, KVH, HD).astype(jnp.float32)
    value_heads = vals.reshape(TOK, KVH, HD).astype(jnp.float32)
    scores = jnp.einsum('qgjd,kgd->gjqk', query_heads, key_heads) * HD ** (-0.5)
    posit = jnp.arange(TOK)
    allowed = (doc_row[:, None] == doc_row[None, :]) & (posit[:, None] >= posit[None, :])
    scores = jnp.where(allowed[None, None], scores, -1e+30)
    top = lax.optimization_barrier(jnp.max(scores, axis=-1, keepdims=True))
    expo = jnp.exp(scores - top)
    probs = (expo / lax.optimization_barrier(jnp.sum(expo, axis=-1, keepdims=True))).astype(jnp.bfloat16)
    heads_out = jnp.einsum('gjqk,kgd->qgjd', probs.astype(jnp.float32), value_heads).astype(jnp.bfloat16)
    partial_value = jnp.einsum('qgjd,gjdn->gqn', heads_out.astype(jnp.float32), wo.reshape(KVH, group, HD, D).astype(jnp.float32))
    summed = lax.optimization_barrier(jnp.sum(partial_value.astype(jnp.bfloat16).astype(jnp.float32), axis=0))
    return (values + summed).astype(jnp.bfloat16)

def reference(rollout, document_ids, batch_order, gains, w_query, bias_query, w_kv, bias_value, w_out):
    per_layer = [[] for layer in range(LAYERS)]
    for group_index in range(N_DP):
        for slot in range(MB_DEV):
            micro_id = (group_index * MB_DEV + batch_order[group_index, slot]).astype(jnp.int32)
            current = lax.dynamic_index_in_dim(rollout, micro_id, 0, keepdims=False)
            doc_row = lax.dynamic_index_in_dim(document_ids, micro_id, 0, keepdims=False)
            for layer in range(LAYERS):
                current = layer_apply(current, doc_row, gains[layer], w_query[layer], bias_query[layer], w_kv[layer, 0], w_kv[layer, 1], bias_value[layer], w_out[layer])
                per_layer[layer].append(current)
    return jnp.stack([jnp.stack(items) for items in per_layer])
```

```python
import functools

import jax
import jax.numpy as jnp
from jax import lax
from jax.experimental import pallas as pl
from jax.experimental.pallas import tpu as pltpu
from jax.sharding import PartitionSpec as P

HD = 128
T = 32
NP = 2
LAGS = 3, 1
MESH = pl.DeviceIdType.MESH


def kernel(
    nsec, ndp, x0, doc_row, doc_col, gains, wq, bq, wkv, bv, w_out, out,
    wcat, wall, xg, hb, xn, pb, pr, kb, vb,
    load_sem, gsend, grecv, fsend, frecv, isend, xrecv, csend, crecv, hsend, hrecv,
    psend, precv, nsend, osend, orecv,
):
    s = lax.axis_index("section")
    z = lax.axis_index("dp")
    t = lax.axis_index("tensor")
    h = t // 2
    c = lax.rem(t, 2)
    micro, rows, width = x0.shape
    tokens = doc_row.shape[2]
    qw = wq.shape[1]
    half = width // 2
    piece = half // NP
    per_mb = tokens // T
    per_own = rows // T
    n = micro * per_mb
    heads = qw // HD
    blk = w_out.shape[1]
    unit = w_out.shape[0] // 2
    sib = {"tensor": 2 * h + 1 - c}
    peer = {"tensor": 2 * (1 - h) + c}
    zright = {"dp": lax.rem(z + 1, ndp)}
    zleft = {"dp": lax.rem(z + ndp - 1, ndp)}

    def remote(src, dst, send, recv, device):
        return pltpu.make_async_remote_copy(
            src_ref=src, dst_ref=dst, send_sem=send, recv_sem=recv,
            device_id=device, device_id_type=MESH,
        )

    loads = []
    for k in range(2):
        base = pl.multiple_of(lax.rem(c + k, 2) * half, half)
        dst = pl.ds(k * half, half)
        loads.append((wq.at[pl.ds(base, half)], wcat.at[dst, pl.ds(0, qw)]))
        for m in range(2):
            loads.append((wkv.at[m, pl.ds(base, half)], wcat.at[dst, pl.ds(qw + m * HD, HD)]))
    loads = [pltpu.make_async_copy(a, b, load_sem.at[k]) for k, (a, b) in enumerate(loads)]

    def place(b, u):
        j = lax.rem(b, 4)
        mine = (b // 4) == c
        slot = jnp.where(mine, j, 4 + j // 2)
        row = jnp.where(mine, 0, lax.rem(j, 2) * (2 * unit)) + u * unit
        return wall.at[slot, pl.ds(pl.multiple_of(row, unit), unit)]

    own_block = [
        pltpu.make_async_copy(w_out.at[pl.ds(u * unit, unit)], place(z, u), load_sem.at[6 + u])
        for u in range(2)
    ]
    for cp in own_block + loads:
        cp.start()

    barrier = pltpu.get_barrier_semaphore()
    partners = [{"tensor": lax.rem(t + k, 4)} for k in range(1, 4)] + [zright, zleft]
    partners += [{"section": lax.rem(s + k, nsec)} for k in (1, nsec - 1)]
    for device in partners:
        pl.semaphore_signal(barrier, inc=1, device_id=device, device_id_type=MESH)
    kb[...] = jnp.zeros_like(kb)
    vb[...] = jnp.zeros_like(vb)
    pl.semaphore_wait(barrier, len(partners))

    def ring(flow, b, k, u):
        return remote(
            place(b, u), place(b, u), gsend.at[flow, k, u], grecv.at[flow, k, u],
            zright if flow == 0 else zleft,
        )

    def to_sib(b, u):
        j = lax.rem(b, 4)
        return remote(
            place(b, u), wall.at[j, pl.ds(pl.multiple_of(2 * unit + u * unit, unit), unit)],
            fsend.at[j, u], frecv.at[j, u], sib,
        )

    for u in range(2):
        own_block[u].wait()
        for flow in range(2):
            ring(flow, z, 0, u).start()

        @pl.when((z // 4) != c)
        def _():
            to_sib(z, u).start()

    def first(j, k, dest, p):
        i = j * per_mb + t * per_own + k
        return (
            x0.at[j, pl.ds(k * T, T), pl.ds(dest % 2 * half + p * piece, piece)],
            xg.at[i, 0, :, pl.ds(p * piece, piece)],
            isend.at[j * per_own + k, dest, p],
            xrecv.at[i, p],
        )

    def firsts(act):
        for j in range(micro):
            for k in range(per_own):
                for p in range(NP):
                    for dest in range(4):
                        src, dst, ssem, rsem = first(j, k, dest, p)

                        @pl.when(dest == t)
                        def _():
                            if act == "start":
                                pltpu.make_async_copy(src, dst, rsem).start()

                        @pl.when(dest != t)
                        def _():
                            cp = remote(src, dst, ssem, rsem, {"tensor": dest})
                            if act == "start":
                                cp.start()
                            else:
                                cp.wait_send()

    @pl.when(s == 0)
    def _():
        firsts("start")

    for cp in loads:
        cp.wait()

    def relay(i, p):
        cols = pl.ds(p * piece, piece)
        return remote(xg.at[i, 0, :, cols], xg.at[i, 1, :, cols], csend.at[i, p], crecv.at[i, p], sib)

    def share(i):
        return remote(hb.at[i, :, pl.ds(0, qw)], hb.at[i, :, pl.ds(qw, qw)], hsend.at[i], hrecv.at[i], sib)

    def exchange(i, k):
        cols = pl.ds(k * piece, piece)
        return remote(pb.at[i, :, cols], pr.at[i, :, cols], psend.at[i, k], precv.at[i, k], peer)

    def hop(i, p):
        cols = pl.ds(p * piece, piece)
        return remote(
            xn.at[i, :, cols], xg.at[i, 0, :, cols], nsend.at[i, p], xrecv.at[i, p],
            {"section": lax.rem(s + 1, nsec)},
        )

    def pass_on(i, p):
        block = xg.at[i, 0, :, pl.ds(p * piece, piece)]
        pltpu.make_async_copy(block, block, xrecv.at[i, p]).wait()
        relay(i, p).start()

    def phase_a(i):
        j = i // per_mb
        r0 = lax.rem(i, per_mb) * T

        def part(k, p):
            x = xg[i, k, :, pl.ds(p * piece, piece)].astype(jnp.float32)
            col = pl.multiple_of(lax.rem(c + k, 2) * half + p * piece, piece)
            g = gains[:, pl.ds(col, piece)]
            sq = jnp.sum(x * x, axis=1, keepdims=True)
            y = jnp.dot(
                (x * g).astype(jnp.bfloat16),
                wcat[pl.ds(k * half + p * piece, piece), :],
                preferred_element_type=jnp.float32,
            )
            return sq, y

        parts = []
        for p in range(NP):
            if p > 0:
                pass_on(i, p)
            parts.append(part(0, p))
        for p in range(NP):
            relay(i, p).wait_recv()
            parts.append(part(1, p))
        sq = sum(a for a, b in parts)
        scale = lax.rsqrt(sq * (1.0 / width) + 1e-6)
        y = sum(b for a, b in parts) * scale
        q = (y[:, :qw] + bq[...]).astype(jnp.bfloat16)
        r0 = pl.multiple_of(r0, T)
        kb[j, pl.ds(r0, T), :] = y[:, qw : qw + HD].astype(jnp.bfloat16)
        vb[j, pl.ds(r0, T), :] = (y[:, qw + HD :] + bv[...]).astype(jnp.bfloat16)
        qs = jnp.concatenate([q[:, k * HD : (k + 1) * HD] for k in range(heads)], axis=0)
        sc = lax.dot_general(
            qs, kb[j], (((1,), (1,)), ((), ())), preferred_element_type=jnp.float32
        ) * HD ** (-0.5)
        dcol = doc_col[j, pl.ds(r0, T), :]
        drow = doc_row[j]
        rowi = lax.broadcasted_iota(jnp.int32, (T, tokens), 0) + r0
        coli = lax.broadcasted_iota(jnp.int32, (T, tokens), 1)
        ok = ((dcol == drow) & (rowi >= coli)).astype(jnp.float32)
        ok = jnp.concatenate([ok] * heads, axis=0) > 0.5
        sc = jnp.where(ok, sc, -1e30)
        top = jnp.max(sc, axis=1, keepdims=True)
        ex = jnp.exp(sc - top)
        probs = (ex / jnp.sum(ex, axis=1, keepdims=True)).astype(jnp.bfloat16)
        o = jnp.dot(probs, vb[j], preferred_element_type=jnp.float32).astype(jnp.bfloat16)
        for k in range(heads):
            hb[i, :, pl.ds(k * HD, HD)] = o[k * T : (k + 1) * T]
        share(i).start()

    def phase_b(i):
        share(i).wait_recv()
        lhs = hb[i]
        for k in range(4):
            y = jnp.dot(lhs, wall[k], preferred_element_type=jnp.float32)
            pb[i, :, pl.ds(k * blk, blk)] = y.astype(jnp.bfloat16)
            if (k + 1) * blk % piece == 0:
                exchange(i, k * blk // piece).start()

    def out_copy(i):
        j = i // per_mb
        r0 = lax.rem(i, per_mb) * T
        owner = r0 // rows
        row = pl.multiple_of(lax.rem(r0, rows), T)
        dst = out.at[j, pl.ds(row, T), pl.ds(pl.multiple_of(c * half, half), half)]
        return owner, xn.at[i], dst, orecv.at[j * per_own + row // T]

    def phase_c(i):
        for p in range(NP):
            cols = pl.ds(p * piece, piece)
            exchange(i, p).wait_recv()
            added = pb[i, :, cols].astype(jnp.float32) + pr[i, :, cols].astype(jnp.float32)
            x = xg[i, 0, :, cols].astype(jnp.float32)
            xn[i, :, cols] = (x + added).astype(jnp.bfloat16)

            @pl.when(s < nsec - 1)
            def _():
                hop(i, p).start()

        owner, src, dst, sem = out_copy(i)

        @pl.when(owner == t)
        def _():
            pltpu.make_async_copy(src, dst, sem).start()

        @pl.when(owner == 2 * h + 1 - c)
        def _():
            remote(src, dst, osend.at[i], sem, sib).start()

    per_step = n // 8

    def gather_step(m, carry):
        k = m // 2
        u = lax.rem(m, 2)
        for flow in range(2):

            @pl.when((k < 3) | (u == flow))
            def _():
                b = lax.rem(z + (ndp - 1 - k if flow == 0 else k + 1), ndp)
                ring(flow, b, k, u).wait_recv()

                @pl.when((k < 2) | ((k == 2) & (u == flow)))
                def _():
                    ring(flow, b, k + 1, u).start()

                @pl.when((b // 4) != c)
                def _():
                    to_sib(b, u).start()

        @pl.when(s == 0)
        def _():
            def both(i, q):
                pass_on(i, 0)
                phase_a(i)
                return q

            lax.fori_loop(m * per_step, (m + 1) * per_step, both, 0)

        return carry

    lax.fori_loop(0, 8, gather_step, 0)
    for j in range(4):
        for u in range(2):
            to_sib(4 * c + j, u).wait_recv()

    lag = jnp.where(s == 0, LAGS[0], LAGS[1])

    @pl.when(s > 0)
    def _():
        pass_on(0, 0)

    def main(i, carry):
        @pl.when((s > 0) & (i < n))
        def _():
            phase_a(i)

        @pl.when(i < n)
        def _():
            phase_b(i)

        @pl.when((s > 0) & (i + 1 < n))
        def _():
            pass_on(i + 1, 0)

        @pl.when(i >= lag)
        def _():
            phase_c(i - lag)

        return carry

    lax.fori_loop(0, n + lag, main, 0)

    for k in range(4):
        for u in range(2):
            for flow in range(2):
                if k < 3 or u == flow:
                    ring(flow, z, k, u).wait_send()
    for j in range(4):
        for u in range(2):
            to_sib(4 * (1 - c) + j, u).wait_send()

    @pl.when(s == 0)
    def _():
        firsts("wait")

    def drain(i, carry):
        share(i).wait_send()
        for k in range(NP):
            relay(i, k).wait_send()
            exchange(i, k).wait_send()

            @pl.when(s < nsec - 1)
            def _():
                hop(i, k).wait_send()

        owner, src, dst, sem = out_copy(i)

        @pl.when(owner == 2 * h + 1 - c)
        def _():
            remote(src, dst, osend.at[i], sem, sib).wait_send()

        return carry

    lax.fori_loop(0, n, drain, 0)
    for j in range(micro):
        for k in range(per_own):
            dst = out.at[j, pl.ds(k * T, T)]
            pltpu.make_async_copy(dst, dst, orecv.at[j * per_own + k]).wait()


def local(nsec, ndp, rollout, document_ids, batch_order, gains, w_query, bias_query, w_kv, bias_value, w_out):
    micro, rows, width = rollout.shape
    tokens = document_ids.shape[1]
    swap = batch_order[0, 0] == 1
    x0 = jnp.where(swap, rollout[::-1], rollout)
    docs = jnp.where(swap, document_ids[::-1], document_ids)
    wq = w_query[0]
    wkv = w_kv[0]
    wo = w_out[0]
    qw = wq.shape[1]
    n = micro * tokens // T
    own = micro * rows // T
    vmem = pl.BlockSpec(memory_space=pltpu.VMEM)
    hbm = pl.BlockSpec(memory_space=pl.ANY)
    bf16 = jnp.bfloat16
    dma = pltpu.SemaphoreType.DMA
    out = pl.pallas_call(
        functools.partial(kernel, nsec, ndp),
        out_shape=jax.ShapeDtypeStruct((micro, rows, width), bf16),
        in_specs=[hbm, vmem, vmem, vmem, hbm, vmem, hbm, vmem, hbm],
        out_specs=hbm,
        scratch_shapes=[
            pltpu.VMEM((width, qw + 2 * HD), bf16),
            pltpu.VMEM((6, 2 * wo.shape[0], wo.shape[1]), bf16),
            pltpu.VMEM((n, 2, T, width // 2), bf16),
            pltpu.VMEM((n, T, 2 * qw), bf16),
            pltpu.VMEM((n, T, width // 2), bf16),
            pltpu.VMEM((n, T, width // 2), bf16),
            pltpu.VMEM((n, T, width // 2), bf16),
            pltpu.VMEM((micro, tokens, HD), bf16),
            pltpu.VMEM((micro, tokens, HD), bf16),
            dma((8,)),
            dma((2, 4, 2)),
            dma((2, 4, 2)),
            dma((4, 2)),
            dma((4, 2)),
            dma((own, 4, NP)),
            dma((n, NP)),
            dma((n, NP)),
            dma((n, NP)),
            dma((n,)),
            dma((n,)),
            dma((n, NP)),
            dma((n, NP)),
            dma((n, NP)),
            dma((n,)),
            dma((own,)),
        ],
        compiler_params=pltpu.CompilerParams(
            collective_id=0, has_side_effects=True, vmem_limit_bytes=48 * 2**20
        ),
        name="layers",
    )(
        x0, docs[:, None, :], docs[:, :, None], gains, wq, bias_query, wkv, bias_value, wo
    )
    return out[None]


def solution(mesh):
    in_specs = (
        P("dp", "tensor", None),
        P("dp", None),
        P("dp", None),
        P("section", None),
        P("section", None, "tensor"),
        P("section", "tensor"),
        P("section", None, None, "tensor"),
        P("section", "tensor"),
        P("section", "tensor", "dp"),
    )
    out_specs = P("section", "dp", "tensor", None)
    body = functools.partial(local, mesh.shape["section"], mesh.shape["dp"])
    return jax.shard_map(body, mesh=mesh, in_specs=in_specs, out_specs=out_specs, check_vma=False)
```

```python
import functools

import jax
import jax.numpy as jnp
from jax import lax
from jax.experimental import pallas as pl
from jax.experimental.pallas import tpu as pltpu
from jax.sharding import PartitionSpec as P

HD = 128
T = 32
NP = 2
LAGS = 3, 1
MESH = pl.DeviceIdType.MESH


def kernel(
    nsec, ndp, rollout, order, doc_row, doc_col, gains, wq, bq, wkv, bv, w_out, out,
    xin, x0, wcat, wall, xg, hb, xn, pb, pr, kb, vb,
    load_sem, gsend, grecv, fsend, frecv, isend, xrecv, csend, crecv, hsend, hrecv,
    psend, precv, nsend, osend, orecv,
):
    s = lax.axis_index("section")
    z = lax.axis_index("dp")
    t = lax.axis_index("tensor")
    h = t // 2
    c = lax.rem(t, 2)
    micro, rows, width = x0.shape
    tokens = doc_row.shape[2]
    qw = wq.shape[1]
    half = width // 2
    piece = half // NP
    per_mb = tokens // T
    per_own = rows // T
    n = micro * per_mb
    heads = qw // HD
    blk = w_out.shape[1]
    unit = w_out.shape[0] // 2
    sib = {"tensor": 2 * h + 1 - c}
    peer = {"tensor": 2 * (1 - h) + c}
    zright = {"dp": lax.rem(z + 1, ndp)}
    zleft = {"dp": lax.rem(z + ndp - 1, ndp)}

    def remote(src, dst, send, recv, device):
        return pltpu.make_async_remote_copy(
            src_ref=src, dst_ref=dst, send_sem=send, recv_sem=recv,
            device_id=device, device_id_type=MESH,
        )

    loads = []
    for k in range(2):
        base = pl.multiple_of(lax.rem(c + k, 2) * half, half)
        dst = pl.ds(k * half, half)
        loads.append((wq.at[pl.ds(base, half)], wcat.at[dst, pl.ds(0, qw)]))
        for m in range(2):
            loads.append((wkv.at[m, pl.ds(base, half)], wcat.at[dst, pl.ds(qw + m * HD, HD)]))
    loads = [pltpu.make_async_copy(a, b, load_sem.at[k]) for k, (a, b) in enumerate(loads)]

    def place(b, u):
        j = lax.rem(b, 4)
        mine = (b // 4) == c
        slot = jnp.where(mine, j, 4 + j // 2)
        row = jnp.where(mine, 0, lax.rem(j, 2) * (2 * unit)) + u * unit
        return wall.at[slot, pl.ds(pl.multiple_of(row, unit), unit)]

    own_block = [
        pltpu.make_async_copy(w_out.at[pl.ds(u * unit, unit)], place(z, u), load_sem.at[6 + u])
        for u in range(2)
    ]
    for cp in own_block + loads:
        cp.start()

    barrier = pltpu.get_barrier_semaphore()
    partners = [{"tensor": lax.rem(t + k, 4)} for k in range(1, 4)] + [zright, zleft]
    partners += [{"section": lax.rem(s + k, nsec)} for k in (1, nsec - 1)]
    for device in partners:
        pl.semaphore_signal(barrier, inc=1, device_id=device, device_id_type=MESH)
    kb[...] = jnp.zeros_like(kb)
    vb[...] = jnp.zeros_like(vb)
    pl.semaphore_wait(barrier, len(partners))

    def ring(flow, b, k, u):
        return remote(
            place(b, u), place(b, u), gsend.at[flow, k, u], grecv.at[flow, k, u],
            zright if flow == 0 else zleft,
        )

    def to_sib(b, u):
        j = lax.rem(b, 4)
        return remote(
            place(b, u), wall.at[j, pl.ds(pl.multiple_of(2 * unit + u * unit, unit), unit)],
            fsend.at[j, u], frecv.at[j, u], sib,
        )

    for u in range(2):
        own_block[u].wait()
        for flow in range(2):
            ring(flow, z, 0, u).start()

        @pl.when((z // 4) != c)
        def _():
            to_sib(z, u).start()

    def first(j, k, dest, p):
        i = j * per_mb + t * per_own + k
        return (
            x0.at[j, pl.ds(k * T, T), pl.ds(dest % 2 * half + p * piece, piece)],
            xg.at[i, 0, :, pl.ds(p * piece, piece)],
            isend.at[j * per_own + k, dest, p],
            xrecv.at[i, p],
        )

    def firsts(act):
        for j in range(micro):
            for k in range(per_own):
                for p in range(NP):
                    for dest in range(4):
                        src, dst, ssem, rsem = first(j, k, dest, p)

                        @pl.when(dest == t)
                        def _():
                            if act == "start":
                                pltpu.make_async_copy(src, dst, rsem).start()

                        @pl.when(dest != t)
                        def _():
                            cp = remote(src, dst, ssem, rsem, {"tensor": dest})
                            if act == "start":
                                cp.start()
                            else:
                                cp.wait_send()

    @pl.when(s == 0)
    def _():
        cp = pltpu.make_async_copy(rollout, xin, load_sem.at[8])
        cp.start()
        cp.wait()
        for j in range(micro):
            x0[j] = xin[order[0, j]]
        firsts("start")

    for cp in loads:
        cp.wait()

    def relay(i, p):
        cols = pl.ds(p * piece, piece)
        return remote(xg.at[i, 0, :, cols], xg.at[i, 1, :, cols], csend.at[i, p], crecv.at[i, p], sib)

    def share(i):
        return remote(hb.at[i, :, pl.ds(0, qw)], hb.at[i, :, pl.ds(qw, qw)], hsend.at[i], hrecv.at[i], sib)

    def exchange(i, k):
        cols = pl.ds(k * piece, piece)
        return remote(pb.at[i, :, cols], pr.at[i, :, cols], psend.at[i, k], precv.at[i, k], peer)

    def hop(i, p):
        cols = pl.ds(p * piece, piece)
        return remote(
            xn.at[i, :, cols], xg.at[i, 0, :, cols], nsend.at[i, p], xrecv.at[i, p],
            {"section": lax.rem(s + 1, nsec)},
        )

    def pass_on(i, p):
        block = xg.at[i, 0, :, pl.ds(p * piece, piece)]
        pltpu.make_async_copy(block, block, xrecv.at[i, p]).wait()
        relay(i, p).start()

    def phase_a(i):
        j = i // per_mb
        r0 = lax.rem(i, per_mb) * T

        def part(k, p):
            x = xg[i, k, :, pl.ds(p * piece, piece)].astype(jnp.float32)
            col = pl.multiple_of(lax.rem(c + k, 2) * half + p * piece, piece)
            g = gains[:, pl.ds(col, piece)]
            sq = jnp.sum(x * x, axis=1, keepdims=True)
            y = jnp.dot(
                (x * g).astype(jnp.bfloat16),
                wcat[pl.ds(k * half + p * piece, piece), :],
                preferred_element_type=jnp.float32,
            )
            return sq, y

        parts = []
        for p in range(NP):
            if p > 0:
                pass_on(i, p)
            parts.append(part(0, p))
        for p in range(NP):
            relay(i, p).wait_recv()
            parts.append(part(1, p))
        sq = sum(a for a, b in parts)
        scale = lax.rsqrt(sq * (1.0 / width) + 1e-6)
        y = sum(b for a, b in parts) * scale
        q = (y[:, :qw] + bq[...]).astype(jnp.bfloat16)
        r0 = pl.multiple_of(r0, T)
        kb[j, pl.ds(r0, T), :] = y[:, qw : qw + HD].astype(jnp.bfloat16)
        vb[j, pl.ds(r0, T), :] = (y[:, qw + HD :] + bv[...]).astype(jnp.bfloat16)
        qs = jnp.concatenate([q[:, k * HD : (k + 1) * HD] for k in range(heads)], axis=0)
        sc = lax.dot_general(
            qs, kb[j], (((1,), (1,)), ((), ())), preferred_element_type=jnp.float32
        ) * HD ** (-0.5)
        dcol = doc_col[j, pl.ds(r0, T), :]
        drow = doc_row[j]
        rowi = lax.broadcasted_iota(jnp.int32, (T, tokens), 0) + r0
        coli = lax.broadcasted_iota(jnp.int32, (T, tokens), 1)
        ok = ((dcol == drow) & (rowi >= coli)).astype(jnp.float32)
        ok = jnp.concatenate([ok] * heads, axis=0) > 0.5
        sc = jnp.where(ok, sc, -1e30)
        top = jnp.max(sc, axis=1, keepdims=True)
        ex = jnp.exp(sc - top)
        probs = (ex / jnp.sum(ex, axis=1, keepdims=True)).astype(jnp.bfloat16)
        o = jnp.dot(probs, vb[j], preferred_element_type=jnp.float32).astype(jnp.bfloat16)
        for k in range(heads):
            hb[i, :, pl.ds(k * HD, HD)] = o[k * T : (k + 1) * T]
        share(i).start()

    def phase_b(i):
        share(i).wait_recv()
        lhs = hb[i]
        for k in range(4):
            y = jnp.dot(lhs, wall[k], preferred_element_type=jnp.float32)
            pb[i, :, pl.ds(k * blk, blk)] = y.astype(jnp.bfloat16)
            if (k + 1) * blk % piece == 0:
                exchange(i, k * blk // piece).start()

    def out_copy(i):
        j = i // per_mb
        r0 = lax.rem(i, per_mb) * T
        owner = r0 // rows
        row = pl.multiple_of(lax.rem(r0, rows), T)
        dst = out.at[j, pl.ds(row, T), pl.ds(pl.multiple_of(c * half, half), half)]
        return owner, xn.at[i], dst, orecv.at[j * per_own + row // T]

    def phase_c(i):
        for p in range(NP):
            cols = pl.ds(p * piece, piece)
            exchange(i, p).wait_recv()
            added = pb[i, :, cols].astype(jnp.float32) + pr[i, :, cols].astype(jnp.float32)
            x = xg[i, 0, :, cols].astype(jnp.float32)
            xn[i, :, cols] = (x + added).astype(jnp.bfloat16)

            @pl.when(s < nsec - 1)
            def _():
                hop(i, p).start()

        owner, src, dst, sem = out_copy(i)

        @pl.when(owner == t)
        def _():
            pltpu.make_async_copy(src, dst, sem).start()

        @pl.when(owner == 2 * h + 1 - c)
        def _():
            remote(src, dst, osend.at[i], sem, sib).start()

    per_step = n // 8

    def gather_step(m, carry):
        k = m // 2
        u = lax.rem(m, 2)
        for flow in range(2):

            @pl.when((k < 3) | (u == flow))
            def _():
                b = lax.rem(z + (ndp - 1 - k if flow == 0 else k + 1), ndp)
                ring(flow, b, k, u).wait_recv()

                @pl.when((k < 2) | ((k == 2) & (u == flow)))
                def _():
                    ring(flow, b, k + 1, u).start()

                @pl.when((b // 4) != c)
                def _():
                    to_sib(b, u).start()

        @pl.when(s == 0)
        def _():
            def both(i, q):
                pass_on(i, 0)
                phase_a(i)
                return q

            lax.fori_loop(m * per_step, (m + 1) * per_step, both, 0)

        return carry

    lax.fori_loop(0, 8, gather_step, 0)
    for j in range(4):
        for u in range(2):
            to_sib(4 * c + j, u).wait_recv()

    lag = jnp.where(s == 0, LAGS[0], LAGS[1])

    @pl.when(s > 0)
    def _():
        pass_on(0, 0)

    def main(i, carry):
        @pl.when((s > 0) & (i < n))
        def _():
            phase_a(i)

        @pl.when(i < n)
        def _():
            phase_b(i)

        @pl.when((s > 0) & (i + 1 < n))
        def _():
            pass_on(i + 1, 0)

        @pl.when(i >= lag)
        def _():
            phase_c(i - lag)

        return carry

    lax.fori_loop(0, n + lag, main, 0)

    for k in range(4):
        for u in range(2):
            for flow in range(2):
                if k < 3 or u == flow:
                    ring(flow, z, k, u).wait_send()
    for j in range(4):
        for u in range(2):
            to_sib(4 * (1 - c) + j, u).wait_send()

    @pl.when(s == 0)
    def _():
        firsts("wait")

    def drain(i, carry):
        share(i).wait_send()
        for k in range(NP):
            relay(i, k).wait_send()
            exchange(i, k).wait_send()

            @pl.when(s < nsec - 1)
            def _():
                hop(i, k).wait_send()

        owner, src, dst, sem = out_copy(i)

        @pl.when(owner == 2 * h + 1 - c)
        def _():
            remote(src, dst, osend.at[i], sem, sib).wait_send()

        return carry

    lax.fori_loop(0, n, drain, 0)
    for j in range(micro):
        for k in range(per_own):
            dst = out.at[j, pl.ds(k * T, T)]
            pltpu.make_async_copy(dst, dst, orecv.at[j * per_own + k]).wait()


def local(nsec, ndp, rollout, document_ids, batch_order, gains, w_query, bias_query, w_kv, bias_value, w_out):
    micro, rows, width = rollout.shape
    tokens = document_ids.shape[1]
    swap = batch_order[0, 0] == 1
    docs = jnp.where(swap, document_ids[::-1], document_ids)
    wq = w_query[0]
    wkv = w_kv[0]
    wo = w_out[0]
    qw = wq.shape[1]
    n = micro * tokens // T
    own = micro * rows // T
    vmem = pl.BlockSpec(memory_space=pltpu.VMEM)
    hbm = pl.BlockSpec(memory_space=pl.ANY)
    bf16 = jnp.bfloat16
    dma = pltpu.SemaphoreType.DMA
    out = pl.pallas_call(
        functools.partial(kernel, nsec, ndp),
        out_shape=jax.ShapeDtypeStruct((micro, rows, width), bf16),
        in_specs=[hbm, pl.BlockSpec(memory_space=pltpu.SMEM), vmem, vmem, vmem, hbm, vmem, hbm, vmem, hbm],
        out_specs=hbm,
        scratch_shapes=[
            pltpu.VMEM((micro, rows, width), bf16),
            pltpu.VMEM((micro, rows, width), bf16),
            pltpu.VMEM((width, qw + 2 * HD), bf16),
            pltpu.VMEM((6, 2 * wo.shape[0], wo.shape[1]), bf16),
            pltpu.VMEM((n, 2, T, width // 2), bf16),
            pltpu.VMEM((n, T, 2 * qw), bf16),
            pltpu.VMEM((n, T, width // 2), bf16),
            pltpu.VMEM((n, T, width // 2), bf16),
            pltpu.VMEM((n, T, width // 2), bf16),
            pltpu.VMEM((micro, tokens, HD), bf16),
            pltpu.VMEM((micro, tokens, HD), bf16),
            dma((9,)),
            dma((2, 4, 2)),
            dma((2, 4, 2)),
            dma((4, 2)),
            dma((4, 2)),
            dma((own, 4, NP)),
            dma((n, NP)),
            dma((n, NP)),
            dma((n, NP)),
            dma((n,)),
            dma((n,)),
            dma((n, NP)),
            dma((n, NP)),
            dma((n, NP)),
            dma((n,)),
            dma((own,)),
        ],
        compiler_params=pltpu.CompilerParams(
            collective_id=0, has_side_effects=True, vmem_limit_bytes=48 * 2**20
        ),
        name="layers",
    )(
        rollout, batch_order, docs[:, None, :], docs[:, :, None], gains, wq, bias_query, wkv, bias_value, wo
    )
    return out[None]


def solution(mesh):
    in_specs = (
        P("dp", "tensor", None),
        P("dp", None),
        P("dp", None),
        P("section", None),
        P("section", None, "tensor"),
        P("section", "tensor"),
        P("section", None, None, "tensor"),
        P("section", "tensor"),
        P("section", "tensor", "dp"),
    )
    out_specs = P("section", "dp", "tensor", None)
    body = functools.partial(local, mesh.shape["section"], mesh.shape["dp"])
    return jax.shard_map(body, mesh=mesh, in_specs=in_specs, out_specs=out_specs, check_vma=False)
```
